1024 devices in a mesh: dp: 16 (over z_hi, x), section: 8 (over z_lo, core), tensor: 8 (over y).
Axes of the slice: x: 8, y: 8, z: 8 (z_hi: 2, z_lo: 4; z = z_hi * 4 + z_lo), core: 2. Of those that a mesh axis runs over, the one named last changes fastest.
Arguments:
- section_inputs: bfloat16 [8, 2, 4096, 8192], P('section', None, 'dp', 'tensor'), may hold values from -6 to 6
- out_grad: bfloat16 [2, 4096, 8192], P(None, 'dp', 'tensor'), may hold values from -6 to 6
- layer_gain: float32 [8, 8192], P('section', 'tensor'), may hold values from 0.6 to 1.2
- init_factor: float32 [8, 8192, 128], P('section', 'tensor'), may hold values from -0.0625 to 0.0625
Outputs:
- sent_grads: bfloat16 [8, 2, 4096, 8192], P('section', None, 'dp', 'tensor')
- residue_out: float32 [8, 4096, 8192], P('section', 'dp', 'tensor')
- gain_grad: float32 [8, 8192], P('section', 'tensor')
The draws below stay inside these ranges and needn't reach their ends.
All inputs are finite; a program needn't handle non-finite values.
Results may differ from the reference program's by a relative error of at most 0.003.
Values sent between devices are 32-bit elements; how exact they have to be, the bound alone decides.
No kernel may reach another device: no remote copies, remote signals or barrier semaphores. Data moves between devices by JAX's collectives and lax.ppermute only.
A program may use at most 32 MiB of HBM per device.

```python
import jax
import jax.numpy as jnp
from jax import lax

D = 8192
R = 128
TOK_DEV = 256
MB = 2
TOKENS = 4096
LAYERS = 8
N_DP = 16


def steps_of(rng, shape, pieces, smallest, high):
    level, own = 1.0, jax.random.fold_in(rng, 6)
    for dim, blocks in pieces:
        draws = jnp.exp(jax.random.uniform(jax.random.fold_in(own, dim), (blocks,), jnp.float32, smallest / len(pieces), high / len(pieces)))
        level = level * jnp.repeat(draws, shape[dim] // blocks).reshape([-1 if axis == dim else 1 for axis in range(len(shape))])
    return level


def scatter_about(rng, shape, scale, reach, cuts=(), kind=jnp.bfloat16):
    entries = jax.random.normal(rng, shape, jnp.float32) * scale
    if len(cuts) > 0:
        entries = steps_of(rng, shape, cuts, -0.22, 0.18) * entries
    return jnp.clip(entries, min=-reach, max=reach).astype(kind)


def setup_inputs(seed: int = 0) -> dict:
    keys = jax.random.split(jax.random.key(seed), 5)
    return {
        "section_inputs": scatter_about(keys[0], (LAYERS, MB, TOKENS, D), 1.0, 6.0, ((0, 8), (2, 16), (3, 8))),
        "out_grad": scatter_about(keys[1], (MB, TOKENS, D), 1.0, 6.0, ((1, 16), (2, 8))),
        "layer_gain": jnp.clip(0.6 + 0.6 * jax.random.uniform(keys[2], (LAYERS, D), jnp.float32) ** steps_of(keys[2], (LAYERS, D), ((0, 8), (1, 8)), -0.2, 0.2), 0.6, 1.2),
        "init_factor": scatter_about(keys[3], (LAYERS, D, R), D ** -0.5, 0.0625, ((0, 8), (1, 8)), jnp.float32),
    }


def compress(merged, basis):
    proj = jnp.einsum('ptd,dr->ptr', merged, basis, precision=lax.Precision.HIGHEST)
    gram = jnp.einsum('ptr,pts->prs', proj, proj, precision=lax.Precision.HIGHEST)
    lower = jnp.linalg.cholesky(gram)
    ortho = lax.linalg.triangular_solve(lower, proj, left_side=False, lower=True, transpose_a=True)
    factor_q = jnp.einsum('ptd,ptr->pdr', merged, ortho, precision=lax.Precision.HIGHEST)
    approx = jnp.einsum('ptr,pdr->ptd', ortho, factor_q, precision=lax.Precision.HIGHEST)
    return (approx, merged - approx)

def reference(section_inputs, out_grad, layer_gain, init_factor):
    inputs = section_inputs.reshape(LAYERS, MB, N_DP, TOK_DEV, D)
    residues = [jnp.zeros((N_DP, TOK_DEV, D), jnp.float32) for layer in range(LAYERS)]
    gain_terms = [jnp.zeros((D,), jnp.float32) for layer in range(LAYERS)]
    sent = [[None] * MB for layer in range(LAYERS)]
    for micro in range(MB):
        upstream = out_grad[micro].reshape(N_DP, TOK_DEV, D).astype(jnp.float32)
        for layer in range(LAYERS - 1, -1, -1):
            saved = inputs[layer, micro].astype(jnp.float32)
            soft = jnp.tanh(saved)
            local = upstream * layer_gain[layer] * (1.0 + soft * soft)
            gain_terms[layer] = gain_terms[layer] + lax.optimization_barrier(jnp.sum(upstream * (2.0 * saved - soft), axis=(0, 1)))
            sent[layer][micro] = local.astype(jnp.bfloat16).reshape(TOKENS, D)
            merged = local + residues[layer]
            approx, residues[layer] = compress(merged, init_factor[layer])
            upstream = approx
    sent_grads = jnp.stack([jnp.stack(sent[layer], axis=0) for layer in range(LAYERS)], axis=0)
    residue_out = jnp.stack([residues[layer].reshape(TOKENS, D) for layer in range(LAYERS)], axis=0)
    scale = 1.0 / jnp.sqrt(jnp.float32(MB * TOKENS))
    gain_grad = jnp.stack(gain_terms, axis=0) * scale
    return (sent_grads, residue_out, gain_grad)
```

```python
import jax
import jax.numpy as jnp
from jax import lax
from jax.sharding import PartitionSpec as P

HIGH = lax.Precision.HIGH
HIGHEST = lax.Precision.HIGHEST


def dot(left, right, over, precision):
    return lax.dot_general(
        left,
        right,
        (over, ((), ())),
        preferred_element_type=jnp.float32,
        precision=precision,
    )


def summed_over(array, axis):
    size = lax.axis_size(axis)
    rows, cols = array.shape
    chunks = lax.all_to_all(array.reshape(size, rows // size, cols), axis, 0, 0)
    mine = jnp.sum(chunks, axis=0)
    copies = jnp.broadcast_to(mine[None], (size, rows // size, cols))
    return lax.all_to_all(copies, axis, 0, 0).reshape(rows, cols)


def body(section_inputs, out_grad, layer_gain, init_factor):
    sections = lax.axis_size("section")
    section = lax.axis_index("section")
    micros = section_inputs.shape[1]
    rows = section_inputs.shape[2]
    width = section_inputs.shape[3]
    rank = init_factor.shape[2]
    basis = init_factor[0]
    is_last = section == sections - 1

    saved = section_inputs[0].astype(jnp.float32)
    soft = jnp.tanh(saved)
    weight = layer_gain * (1.0 + soft * soft)
    slope = 2.0 * saved - soft

    factor_m = jnp.zeros((rows, rank), jnp.float32)
    factor_q = jnp.zeros((width, rank), jnp.float32)
    residue = jnp.zeros((rows, width), jnp.float32)
    gain_total = jnp.zeros((width,), jnp.float32)
    sent = [jnp.zeros((rows, width), jnp.bfloat16) for _ in range(micros)]

    def pick(array, micro):
        return lax.dynamic_index_in_dim(array, micro, 0, keepdims=False)

    for stage in range(sections + micros - 1):
        micro = stage - (sections - 1 - section)
        active = (micro >= 0) & (micro < micros)
        micro = jnp.clip(micro, 0, micros - 1)
        upstream = dot(factor_m, factor_q, ((1,), (1,)), HIGH)
        if stage < micros:
            upstream = jnp.where(is_last, out_grad[stage].astype(jnp.float32), upstream)
        local = upstream * pick(weight, micro)
        merged = local + residue
        partial = dot(merged, basis, ((1,), (0,)), HIGH)
        proj = summed_over(partial, "tensor")
        gain_total += jnp.where(active, jnp.sum(upstream * pick(slope, micro), axis=0), 0.0)
        for m in range(micros):
            sent[m] = jnp.where(active & (micro == m), local.astype(jnp.bfloat16), sent[m])
        pairs = [
            (s, s - 1)
            for s in range(1, sections)
            if 0 <= stage - (sections - 1 - s) < micros
        ]
        out_q = dot(merged, proj, ((0,), (0,)), HIGH)
        if pairs:
            factor_q = lax.ppermute(out_q, "section", pairs)
        gram = dot(proj, proj, ((0,), (0,)), HIGHEST)
        lower = jnp.linalg.cholesky(gram)
        inverse = lax.linalg.triangular_solve(
            lower, jnp.eye(rank, dtype=jnp.float32), left_side=True, lower=True
        )
        ortho = dot(proj, inverse, ((1,), (1,)), HIGHEST)
        out_m = dot(ortho, inverse, ((1,), (0,)), HIGHEST)
        if pairs:
            factor_m = lax.ppermute(out_m, "section", pairs)
        residue = jnp.where(active, merged - dot(out_m, out_q, ((1,), (1,)), HIGH), residue)

    n_dp = lax.axis_size("dp")
    gathered = lax.all_to_all(
        jnp.broadcast_to(gain_total.reshape(1, 8, width // 8), (n_dp, 8, width // 8)), "dp", 0, 0
    )
    summed = jnp.sum(gathered, axis=0).reshape(width)
    gain_grad = summed * (1.0 / jnp.sqrt(jnp.float32(micros * rows * n_dp)))
    return (jnp.stack(sent)[None], residue[None], gain_grad[None])


def solution(mesh):
    placed = (
        P("section", None, "dp", "tensor"),
        P(None, "dp", "tensor"),
        P("section", "tensor"),
        P("section", "tensor", None),
    )
    return jax.shard_map(
        body,
        mesh=mesh,
        in_specs=placed,
        out_specs=(
            P("section", None, "dp", "tensor"),
            P("section", "dp", "tensor"),
            P("section", "tensor"),
        ),
        check_vma=False,
    )
```

```python
import functools

import jax
import jax.numpy as jnp
from jax import lax
from jax.experimental import pallas as pl
from jax.experimental.pallas import tpu as pltpu
from jax.sharding import PartitionSpec as P

HIGHEST = lax.Precision.HIGHEST
VMEM = pltpu.VMEM
PANEL = 16
BLOCK = 512


def dot(left, right, over, precision=None):
    return lax.dot_general(
        left,
        right,
        (over, ((), ())),
        preferred_element_type=jnp.float32,
        precision=precision,
    )


def halves(array):
    high = array.astype(jnp.bfloat16)
    return high, (array - high.astype(jnp.float32)).astype(jnp.bfloat16)


def product(left_pair, right_pair):
    lh, ll = left_pair
    rh, rl = right_pair
    over = ((1,), (0,))
    return dot(lh, rh, over) + (dot(ll, rh, over) + dot(lh, rl, over))


def front_kernel(mode, info, *refs):
    refs = list(refs)
    m_ref, q_ref = (refs.pop(0), refs.pop(0)) if mode > 0 else (None, None)
    grad_ref = refs.pop(0) if mode < 2 else None
    res_ref = refs.pop(0) if mode > 0 else None
    saved_ref, gain_ref, basis_ref, total_ref = refs[:4]
    partial_ref, merged_ref, total_out, sent_ref, local_buf, sems = refs[5:]
    micro, active, is_last = info[0], info[1], info[2]
    width = merged_ref.shape[1]
    rank = partial_ref.shape[1]
    keep = (active > 0).astype(jnp.float32)
    pair_m = halves(m_ref[...]) if mode > 0 else None
    acc = None

    def store(lo):
        cols = pl.ds(lo, BLOCK)
        return pltpu.make_async_copy(
            local_buf.at[:, cols], sent_ref.at[micro, :, cols], sems.at[lo // BLOCK]
        )

    for lo in range(0, width, BLOCK):
        cols = pl.ds(lo, BLOCK)
        if mode > 0:
            up = product(pair_m, halves(q_ref[:, cols]))
        if mode < 2:
            given = grad_ref[:, cols].astype(jnp.float32)
            up = given if mode == 0 else jnp.where(is_last > 0, given, up)
        saved = saved_ref[micro, :, cols].astype(jnp.float32)
        soft = jnp.tanh(saved)
        local = up * gain_ref[:, cols] * (1.0 + soft * soft)
        term = jnp.sum(up * (2.0 * saved - soft), axis=0, keepdims=True)
        total_out[:, cols] = total_ref[:, cols] + jnp.where(keep > 0, term, 0.0)
        local_buf[:, cols] = local.astype(jnp.bfloat16)

        @pl.when(active > 0)
        def _():
            store(lo).start()

        merged = local + res_ref[:, cols] if mode > 0 else local
        merged_ref[:, cols] = merged
        high, low = halves(merged)
        both = basis_ref[pl.ds(lo, BLOCK), :]
        wide = dot(high, both, ((1,), (0,)))
        part = wide[:, :rank] + (wide[:, rank:] + dot(low, both[:, :rank], ((1,), (0,))))
        acc = part if acc is None else acc + part
    partial_ref[...] = acc

    @pl.when(active > 0)
    def _():
        for lo in range(0, width, BLOCK):
            store(lo).wait()


def front(mode, info, m, q, grad, residue, saved, gain, basis, total, sent):
    rows, width = saved.shape[1:]
    rank = basis.shape[1] // 2
    args = []
    if mode > 0:
        args += [m, q]
    if mode < 2:
        args += [grad]
    if mode > 0:
        args += [residue]
    args += [saved, gain, basis, total]
    return pl.pallas_call(
        functools.partial(front_kernel, mode),
        out_shape=(
            jax.ShapeDtypeStruct((rows, rank), jnp.float32),
            jax.ShapeDtypeStruct((rows, width), jnp.float32),
            jax.ShapeDtypeStruct((1, width), jnp.float32),
            jax.ShapeDtypeStruct(sent.shape, sent.dtype),
        ),
        in_specs=[pl.BlockSpec(memory_space=pltpu.SMEM)]
        + [pl.BlockSpec(memory_space=VMEM)] * len(args)
        + [pl.BlockSpec(memory_space=pl.ANY)],
        out_specs=[pl.BlockSpec(memory_space=VMEM)] * 3 + [pl.BlockSpec(memory_space=pl.ANY)],
        input_output_aliases={len(args) + 1: 3},
        scratch_shapes=[
            pltpu.VMEM((rows, width), jnp.bfloat16),
            pltpu.SemaphoreType.DMA((width // BLOCK,)),
        ],
        compiler_params=pltpu.CompilerParams(vmem_limit_bytes=16 << 20),
        cost_estimate=pl.CostEstimate(
            flops=12 * rows * width * rank, bytes_accessed=4 << 20, transcendentals=rows * width
        ),
        name="front",
    )(info, *args, sent)


def factor_kernel(proj_ref, merged_ref, out_ref):
    turned = proj_ref[...].T
    high, low = halves(turned)
    for lo in range(0, merged_ref.shape[1], BLOCK):
        cols = pl.ds(lo, BLOCK)
        out_ref[:, cols] = product((high, low), halves(merged_ref[:, cols]))


def factor(proj, merged):
    rank, width = proj.shape[1], merged.shape[1]
    return pl.pallas_call(
        factor_kernel,
        out_shape=jax.ShapeDtypeStruct((rank, width), jnp.float32),
        in_specs=[pl.BlockSpec(memory_space=VMEM)] * 2,
        out_specs=pl.BlockSpec(memory_space=VMEM),
        compiler_params=pltpu.CompilerParams(vmem_limit_bytes=16 << 20),
        cost_estimate=pl.CostEstimate(
            flops=6 * rank * width * proj.shape[0], bytes_accessed=2 << 20, transcendentals=0
        ),
        name="factor",
    )(proj, merged)


def spread(array, col):
    return jnp.broadcast_to(array[:, col : col + 1], array.shape)


def invert(grid_ref):
    size = grid_ref.shape[0]
    lane = lax.broadcasted_iota(jnp.int32, (PANEL, size), 1)
    row = lax.broadcasted_iota(jnp.int32, (PANEL, size), 0)
    count = size // PANEL
    for k in range(count):
        lo = k * PANEL
        band = grid_ref[lo : lo + PANEL, :]
        inside = (lane >= lo) & (lane < lo + PANEL)
        cols = [spread(band, lo + j) for j in range(PANEL)]
        work = jnp.where(inside, jnp.where(lane - lo == row, 1.0, 0.0), band)
        for j in range(0, PANEL, 2):
            left, right = cols[j], cols[j + 1]
            a, c = left[j : j + 1], left[j + 1 : j + 2]
            b, d = right[j : j + 1], right[j + 1 : j + 2]
            scale = 1.0 / (a * d - b * c)
            ia, ib, ic, id_ = d * scale, -(b * scale), -(c * scale), a * scale
            first, second = row == j, row == j + 1

            def eliminate(block):
                top, low = block[j : j + 1], block[j + 1 : j + 2]
                new_top, new_low = ia * top + ib * low, ic * top + id_ * low
                rest = block - left * new_top - right * new_low
                return jnp.where(first, new_top, jnp.where(second, new_low, rest))

            for q in range(j + 2, PANEL):
                cols[q] = eliminate(cols[q])
            work = eliminate(work)
        for step in range(count - 1):
            at = (k + 1 + step) % count * PANEL
            other = grid_ref[at : at + PANEL, :]
            total = jnp.where(inside, 0.0, other)
            for j in range(PANEL):
                total = total - spread(other, lo + j) * work[j : j + 1]
            grid_ref[at : at + PANEL, :] = total
        grid_ref[lo : lo + PANEL, :] = work


def solve_kernel(proj_ref, out_ref, grid_ref):
    proj = proj_ref[...]
    grid_ref[...] = dot(proj, proj, ((0,), (0,)), HIGHEST)
    invert(grid_ref)
    out_ref[...] = dot(proj, grid_ref[...], ((1,), (0,)), HIGHEST)


def solve(proj):
    rows, rank = proj.shape
    return pl.pallas_call(
        solve_kernel,
        out_shape=jax.ShapeDtypeStruct((rows, rank), jnp.float32),
        in_specs=[pl.BlockSpec(memory_space=VMEM)],
        out_specs=pl.BlockSpec(memory_space=VMEM),
        scratch_shapes=[pltpu.VMEM((rank, rank), jnp.float32)],
        compiler_params=pltpu.CompilerParams(vmem_limit_bytes=16 << 20),
        cost_estimate=pl.CostEstimate(
            flops=3 << 30, bytes_accessed=1 << 18, transcendentals=0
        ),
        name="solve",
    )(proj)


def back_kernel(info, merged_ref, m_ref, q_ref, _last_in, res_ref, last_ref, sem):
    @pl.when(info[1] > 0)
    def _():
        pair_m = halves(m_ref[...])
        for lo in range(0, merged_ref.shape[1], BLOCK):
            cols = pl.ds(lo, BLOCK)
            res_ref[:, cols] = merged_ref[:, cols] - product(pair_m, halves(q_ref[:, cols]))

        @pl.when(info[0] == info[3])
        def _():
            write = pltpu.make_async_copy(res_ref, last_ref, sem)
            write.start()
            write.wait()

    @pl.when(info[1] == 0)
    def _():
        res_ref[...] = jnp.zeros_like(res_ref)


def back(info, merged, m, q, last):
    rows, width = merged.shape
    anywhere = pl.BlockSpec(memory_space=pl.ANY)
    return pl.pallas_call(
        back_kernel,
        out_shape=(jax.ShapeDtypeStruct((rows, width), jnp.float32),) * 2,
        in_specs=[pl.BlockSpec(memory_space=pltpu.SMEM)]
        + [pl.BlockSpec(memory_space=VMEM)] * 3
        + [anywhere],
        out_specs=[pl.BlockSpec(memory_space=VMEM), anywhere],
        input_output_aliases={4: 1},
        scratch_shapes=[pltpu.SemaphoreType.DMA],
        compiler_params=pltpu.CompilerParams(vmem_limit_bytes=16 << 20),
        cost_estimate=pl.CostEstimate(
            flops=6 * rows * width * m.shape[1], bytes_accessed=3 << 20, transcendentals=0
        ),
        name="back",
    )(info, merged, m, q, last)


def summed_over(array, axis):
    size = lax.axis_size(axis)
    rows, cols = array.shape
    chunks = lax.all_to_all(array.reshape(size, rows // size, cols), axis, 0, 0)
    mine = jnp.sum(chunks, axis=0)
    copies = jnp.broadcast_to(mine[None], (size, rows // size, cols))
    return lax.all_to_all(copies, axis, 0, 0).reshape(rows, cols)


def body(section_inputs, out_grad, layer_gain, init_factor):
    sections = lax.axis_size("section")
    section = lax.axis_index("section")
    micros, rows, width = section_inputs.shape[1:]
    saved = section_inputs[0]
    rounded = lax.reduce_precision(init_factor[0], 8, 7)
    basis = jnp.concatenate([rounded, init_factor[0] - rounded], axis=1).astype(jnp.bfloat16)

    m = q = None
    residue = None
    last = jnp.zeros((rows, width), jnp.float32)
    total = jnp.zeros((1, width), jnp.float32)
    sent = jnp.zeros((micros, rows, width), jnp.bfloat16)
    is_last = (section == sections - 1).astype(jnp.int32)

    for stage in range(sections + micros - 1):
        micro = stage - (sections - 1 - section)
        active = ((micro >= 0) & (micro < micros)).astype(jnp.int32)
        info = jnp.stack([jnp.clip(micro, 0, micros - 1), active, is_last, jnp.int32(micros - 1)])
        mode = 0 if stage == 0 else 1 if stage < micros else 2
        grad = out_grad[min(stage, micros - 1)]
        partial, merged, total, sent = front(
            mode, info, m, q, grad, residue, saved, layer_gain, basis, total, sent
        )
        proj = summed_over(partial, "tensor")
        pairs = [
            (s, s - 1)
            for s in range(1, sections)
            if 0 <= stage - (sections - 1 - s) < micros
        ]
        own_q = factor(proj, merged)
        if pairs:
            q = lax.ppermute(own_q, "section", pairs)
        own_m = solve(proj)
        if pairs:
            m = lax.ppermute(own_m, "section", pairs)
        residue, last = back(info, merged, own_m, own_q, last)

    n_dp = lax.axis_size("dp")
    gathered = lax.all_to_all(
        jnp.broadcast_to(total.reshape(1, 8, width // 8), (n_dp, 8, width // 8)), "dp", 0, 0
    )
    summed = jnp.sum(gathered, axis=0).reshape(width)
    gain_grad = summed * (1.0 / jnp.sqrt(jnp.float32(micros * rows * n_dp)))
    return (sent[None], last[None], gain_grad[None])


def solution(mesh):
    placed = (
        P("section", None, "dp", "tensor"),
        P(None, "dp", "tensor"),
        P("section", "tensor"),
        P("section", "tensor", None),
    )
    return jax.shard_map(
        body,
        mesh=mesh,
        in_specs=placed,
        out_specs=(
            P("section", None, "dp", "tensor"),
            P("section", "dp", "tensor"),
            P("section", "tensor"),
        ),
        check_vma=False,
    )
```

```python
import functools

import jax
import jax.numpy as jnp
from jax import lax
from jax.experimental import pallas as pl
from jax.experimental.pallas import tpu as pltpu
from jax.sharding import PartitionSpec as P

HIGHEST = lax.Precision.HIGHEST
VMEM = pltpu.VMEM
PANEL = 16
BLOCK = 512


def dot(left, right, over, precision=None):
    return lax.dot_general(
        left,
        right,
        (over, ((), ())),
        preferred_element_type=jnp.float32,
        precision=precision,
    )


def halves(array):
    high = array.astype(jnp.bfloat16)
    return high, (array - high.astype(jnp.float32)).astype(jnp.bfloat16)


def product(left_pair, right_pair):
    lh, ll = left_pair
    rh, rl = right_pair
    over = ((1,), (0,))
    return dot(lh, rh, over) + (dot(ll, rh, over) + dot(lh, rl, over))


def front_kernel(stage, has_grad, info, *refs):
    refs = list(refs)
    first = stage == 0
    m_ref, q_ref, res_ref = (None,) * 3 if first else [refs.pop(0) for _ in range(3)]
    grad_ref = refs.pop(0) if has_grad else None
    saved_ref, gain_ref, basis_ref = [refs.pop(0) for _ in range(3)]
    total_ref = None if first else refs.pop(0)
    if not first:
        refs.pop(0)
    partial_ref, merged_ref, total_out = [refs.pop(0) for _ in range(3)]
    pair_ref = refs.pop(0) if first else basis_ref
    sent_ref, local_buf, sems = refs
    micro, active, is_last = info[0], info[1], info[2]
    width = merged_ref.shape[1]
    rank = partial_ref.shape[1]
    pair_m = None if first else halves(m_ref[...])
    acc = None

    def store(lo):
        cols = pl.ds(lo, BLOCK)
        return pltpu.make_async_copy(
            local_buf.at[:, cols], sent_ref.at[micro, :, cols], sems.at[lo // BLOCK]
        )

    for lo in range(0, width, BLOCK):
        cols = pl.ds(lo, BLOCK)
        up = None if first else product(pair_m, halves(q_ref[:, cols]))
        if has_grad:
            given = grad_ref[stage, :, cols].astype(jnp.float32)
            up = given if first else jnp.where(is_last > 0, given, up)
        saved = saved_ref[micro, :, cols].astype(jnp.float32)
        soft = jnp.tanh(saved)
        local = up * gain_ref[:, cols] * (1.0 + soft * soft)
        local_buf[:, cols] = local.astype(jnp.bfloat16)

        @pl.when(active > 0)
        def _():
            store(lo).start()

        term = jnp.sum(up * (2.0 * saved - soft), axis=0, keepdims=True)
        term = jnp.where(active > 0, term, 0.0)
        total_out[:, cols] = term if first else total_ref[:, cols] + term
        merged = local if first else local + res_ref[:, cols]
        merged_ref[:, cols] = merged
        high, low = halves(merged)
        if first:
            both = jnp.concatenate(halves(basis_ref[cols, :]), axis=1)
            pair_ref[cols, :] = both
        else:
            both = basis_ref[cols, :]
        wide = dot(high, both, ((1,), (0,)))
        part = wide[:, :rank] + (wide[:, rank:] + dot(low, both[:, :rank], ((1,), (0,))))
        acc = part if acc is None else acc + part
    partial_ref[...] = acc

    @pl.when(active > 0)
    def _():
        for lo in range(0, width, BLOCK):
            store(lo).wait()


def front(stage, info, m, q, residue, grad, saved, gain, basis, total, sent):
    micros, rows, width = saved.shape
    first = stage == 0
    has_grad = stage < micros
    rank = basis.shape[1] if first else basis.shape[1] // 2
    whole, anywhere = pl.BlockSpec(memory_space=VMEM), pl.BlockSpec(memory_space=pl.ANY)
    args = [] if first else [m, q, residue]
    args += [grad] if has_grad else []
    args += [saved, gain, basis]
    args += [] if first else [total]
    specs = [pl.BlockSpec(memory_space=pltpu.SMEM)] + [whole] * len(args)
    shapes = [
        jax.ShapeDtypeStruct((rows, rank), jnp.float32),
        jax.ShapeDtypeStruct((rows, width), jnp.float32),
        jax.ShapeDtypeStruct((1, width), jnp.float32),
    ]
    if first:
        shapes.append(jax.ShapeDtypeStruct((width, 2 * rank), jnp.bfloat16))
    shapes.append(jax.ShapeDtypeStruct(saved.shape, jnp.bfloat16))
    if not first:
        args.append(sent)
        specs.append(anywhere)
    return pl.pallas_call(
        functools.partial(front_kernel, stage, has_grad),
        out_shape=tuple(shapes),
        in_specs=specs,
        out_specs=[whole] * (len(shapes) - 1) + [anywhere],
        input_output_aliases={} if first else {len(args): len(shapes) - 1},
        scratch_shapes=[
            pltpu.VMEM((rows, width), jnp.bfloat16),
            pltpu.SemaphoreType.DMA((width // BLOCK,)),
        ],
        compiler_params=pltpu.CompilerParams(vmem_limit_bytes=24 << 20),
        cost_estimate=pl.CostEstimate(
            flops=12 * rows * width * rank, bytes_accessed=4 << 20, transcendentals=rows * width
        ),
        name="front",
    )(info, *args)


def factor_kernel(proj_ref, merged_ref, out_ref):
    turned = proj_ref[...].T
    high, low = halves(turned)
    for lo in range(0, merged_ref.shape[1], BLOCK):
        cols = pl.ds(lo, BLOCK)
        out_ref[:, cols] = product((high, low), halves(merged_ref[:, cols]))


def factor(proj, merged):
    rank, width = proj.shape[1], merged.shape[1]
    return pl.pallas_call(
        factor_kernel,
        out_shape=jax.ShapeDtypeStruct((rank, width), jnp.float32),
        in_specs=[pl.BlockSpec(memory_space=VMEM)] * 2,
        out_specs=pl.BlockSpec(memory_space=VMEM),
        compiler_params=pltpu.CompilerParams(vmem_limit_bytes=16 << 20),
        cost_estimate=pl.CostEstimate(
            flops=6 * rank * width * proj.shape[0], bytes_accessed=2 << 20, transcendentals=0
        ),
        name="factor",
    )(proj, merged)


def spread(array, col):
    return jnp.broadcast_to(array[:, col : col + 1], array.shape)


def repeated(array, row):
    return jnp.broadcast_to(array[row : row + 1], array.shape)


def eliminate_below(grid_ref, lower_ref):
    size = grid_ref.shape[0]
    lane = lax.broadcasted_iota(jnp.int32, (PANEL, size), 1)
    row = lax.broadcasted_iota(jnp.int32, (PANEL, size), 0)
    for lo in range(0, size, PANEL):
        band = grid_ref[lo : lo + PANEL, :]
        inside = (lane >= lo) & (lane < lo + PANEL)
        upto = lane < lo + PANEL
        cols = [spread(band, lo + j) for j in range(PANEL)]
        work = jnp.where(inside, jnp.where(lane - lo == row, 1.0, 0.0), band)
        lower_ref[lo : lo + PANEL, :] = jnp.where(upto, work, 0.0)
        for j in range(PANEL):
            here = row == j
            scaled = jnp.where(here, -1.0, cols[j]) * (1.0 / repeated(cols[j], j))
            for q in range(j + 1, PANEL):
                cols[q] = jnp.where(here, 0.0, cols[q]) - scaled * repeated(cols[q], j)
            work = jnp.where(here, 0.0, work) - scaled * repeated(work, j)
        for at in range(lo + PANEL, size, PANEL):
            other = grid_ref[at : at + PANEL, :]
            sums = [spread(other, lo + j) * repeated(work, j) for j in range(4)]
            for j in range(4, PANEL):
                sums[j % 4] += spread(other, lo + j) * repeated(work, j)
            taken = (sums[0] + sums[1]) + (sums[2] + sums[3])
            grid_ref[at : at + PANEL, :] = jnp.where(inside, 0.0, other) - taken
        grid_ref[lo : lo + PANEL, :] = jnp.where(upto, work, 0.0)


def solve_kernel(proj_ref, out_ref, grid_ref, lower_ref):
    proj = proj_ref[...]
    grid_ref[...] = dot(proj, proj, ((0,), (0,)), HIGHEST)
    eliminate_below(grid_ref, lower_ref)
    turned = dot(proj, lower_ref[...], ((1,), (1,)), HIGHEST)
    out_ref[...] = dot(turned, grid_ref[...], ((1,), (0,)), HIGHEST)


def solve(proj):
    rows, rank = proj.shape
    return pl.pallas_call(
        solve_kernel,
        out_shape=jax.ShapeDtypeStruct((rows, rank), jnp.float32),
        in_specs=[pl.BlockSpec(memory_space=VMEM)],
        out_specs=pl.BlockSpec(memory_space=VMEM),
        scratch_shapes=[pltpu.VMEM((rank, rank), jnp.float32)] * 2,
        compiler_params=pltpu.CompilerParams(vmem_limit_bytes=16 << 20),
        cost_estimate=pl.CostEstimate(
            flops=3 << 30, bytes_accessed=1 << 18, transcendentals=0
        ),
        name="solve",
    )(proj)


def back_kernel(info, merged_ref, m_ref, q_ref, *refs):
    res_ref, last_ref, sem = refs[-3:]

    @pl.when(info[1] > 0)
    def _():
        pair_m = halves(m_ref[...])
        for lo in range(0, merged_ref.shape[1], BLOCK):
            cols = pl.ds(lo, BLOCK)
            res_ref[:, cols] = merged_ref[:, cols] - product(pair_m, halves(q_ref[:, cols]))

        @pl.when(info[0] == info[3])
        def _():
            write = pltpu.make_async_copy(res_ref, last_ref, sem)
            write.start()
            write.wait()

    @pl.when(info[1] == 0)
    def _():
        res_ref[...] = jnp.zeros_like(res_ref)


def back(info, merged, m, q, last):
    rows, width = merged.shape
    anywhere = pl.BlockSpec(memory_space=pl.ANY)
    held = [] if last is None else [last]
    return pl.pallas_call(
        back_kernel,
        out_shape=(jax.ShapeDtypeStruct((rows, width), jnp.float32),) * 2,
        in_specs=[pl.BlockSpec(memory_space=pltpu.SMEM)]
        + [pl.BlockSpec(memory_space=VMEM)] * 3
        + [anywhere] * len(held),
        out_specs=[pl.BlockSpec(memory_space=VMEM), anywhere],
        input_output_aliases={4: 1} if held else {},
        scratch_shapes=[pltpu.SemaphoreType.DMA],
        compiler_params=pltpu.CompilerParams(vmem_limit_bytes=16 << 20),
        cost_estimate=pl.CostEstimate(
            flops=6 * rows * width * m.shape[1], bytes_accessed=3 << 20, transcendentals=0
        ),
        name="back",
    )(info, merged, m, q, *held)


def summed_over(array, axis):
    size = lax.axis_size(axis)
    rows, cols = array.shape
    chunks = lax.all_to_all(array.reshape(size, rows // size, cols), axis, 0, 0)
    mine = jnp.sum(chunks, axis=0)
    copies = jnp.broadcast_to(mine[None], (size, rows // size, cols))
    return lax.all_to_all(copies, axis, 0, 0).reshape(rows, cols)


def body(section_inputs, out_grad, layer_gain, init_factor):
    sections = lax.axis_size("section")
    section = lax.axis_index("section")
    micros, rows, width = section_inputs.shape[1:]
    saved = section_inputs[0]
    basis = init_factor[0]
    m = q = residue = total = sent = last = None
    is_last = (section == sections - 1).astype(jnp.int32)

    for stage in range(sections + micros - 1):
        micro = stage - (sections - 1 - section)
        active = ((micro >= 0) & (micro < micros)).astype(jnp.int32)
        info = jnp.stack([jnp.clip(micro, 0, micros - 1), active, is_last, jnp.int32(micros - 1)])
        partial, merged, total, *pair, sent = front(
            stage, info, m, q, residue, out_grad, saved, layer_gain, basis, total, sent
        )
        if pair:
            basis = pair[0]
        proj = summed_over(partial, "tensor")
        pairs = [
            (s, s - 1)
            for s in range(1, sections)
            if 0 <= stage - (sections - 1 - s) < micros
        ]
        own_q = factor(proj, merged)
        if pairs:
            q = lax.ppermute(own_q, "section", pairs)
        own_m = solve(proj)
        if pairs:
            m = lax.ppermute(own_m, "section", pairs)
        residue, last = back(info, merged, own_m, own_q, last)

    n_dp = lax.axis_size("dp")
    total = lax.optimization_barrier((total, proj))[0]
    gathered = lax.all_to_all(
        jnp.broadcast_to(total.reshape(1, 8, width // 8), (n_dp, 8, width // 8)), "dp", 0, 0
    )
    summed = jnp.sum(gathered, axis=0).reshape(width)
    gain_grad = summed * (1.0 / jnp.sqrt(jnp.float32(micros * rows * n_dp)))
    return (sent[None], last[None], gain_grad[None])


def solution(mesh):
    placed = (
        P("section", None, "dp", "tensor"),
        P(None, "dp", "tensor"),
        P("section", "tensor"),
        P("section", "tensor", None),
    )
    return jax.shard_map(
        body,
        mesh=mesh,
        in_specs=placed,
        out_specs=(
            P("section", None, "dp", "tensor"),
            P("section", "dp", "tensor"),
            P("section", "tensor"),
        ),
        check_vma=False,
    )
```

```python
import functools

import jax
import jax.numpy as jnp
from jax import lax
from jax.experimental import pallas as pl
from jax.experimental.pallas import tpu as pltpu
from jax.sharding import PartitionSpec as P

HIGHEST = lax.Precision.HIGHEST
VMEM = pltpu.VMEM
PANEL = 16
BLOCK = 512


def dot(left, right, over, precision=None):
    return lax.dot_general(
        left,
        right,
        (over, ((), ())),
        preferred_element_type=jnp.float32,
        precision=precision,
    )


def halves(array):
    high = array.astype(jnp.bfloat16)
    return high, (array - high.astype(jnp.float32)).astype(jnp.bfloat16)


def product(left_pair, right_pair):
    lh, ll = left_pair
    rh, rl = right_pair
    over = ((1,), (0,))
    return dot(lh, rh, over) + (dot(ll, rh, over) + dot(lh, rl, over))


def front_kernel(stage, has_grad, info, *refs):
    refs = list(refs)
    first = stage == 0
    m_ref, q_ref, res_ref = (None,) * 3 if first else [refs.pop(0) for _ in range(3)]
    grad_ref = refs.pop(0) if has_grad else None
    saved_ref, gain_ref, basis_ref = [refs.pop(0) for _ in range(3)]
    total_ref = None if first else refs.pop(0)
    if not first:
        refs.pop(0)
    partial_ref, merged_ref, total_out = [refs.pop(0) for _ in range(3)]
    pair_ref = refs.pop(0) if first else basis_ref
    sent_ref, local_buf, sent_sems = [refs.pop(0) for _ in range(3)]
    micro, active, is_last = info[0], info[1], info[2]
    width = merged_ref.shape[1]
    rank = partial_ref.shape[1]
    blocks = range(0, width, BLOCK)
    copies = []
    if has_grad:
        grad_buf, sems = refs.pop(0), refs.pop()
        copies = [
            [pltpu.make_async_copy(
                grad_ref.at[stage, :, pl.ds(lo, BLOCK)], grad_buf.at[:, pl.ds(lo, BLOCK)],
                sems.at[0, lo // BLOCK],
            )]
            for lo in blocks
        ]
    if first:
        saved_buf, basis_buf = refs
        for lo, several in zip(blocks, copies):
            cols = pl.ds(lo, BLOCK)
            several.append(pltpu.make_async_copy(
                saved_ref.at[micro, :, cols], saved_buf.at[:, cols], sems.at[1, lo // BLOCK]
            ))
            several.append(pltpu.make_async_copy(
                basis_ref.at[cols, :], basis_buf.at[cols, :], sems.at[2, lo // BLOCK]
            ))
    for several in copies:
        for copy in several:
            copy.start()

    def store(lo):
        cols = pl.ds(lo, BLOCK)
        return pltpu.make_async_copy(
            local_buf.at[:, cols], sent_ref.at[micro, :, cols], sent_sems.at[lo // BLOCK]
        )

    pair_m = None if first else halves(m_ref[...])

    for lo in blocks:
        cols = pl.ds(lo, BLOCK)
        up = None if first else product(pair_m, halves(q_ref[:, cols]))
        if has_grad:
            for copy in copies[lo // BLOCK]:
                copy.wait()
            given = grad_buf[:, cols].astype(jnp.float32)
            up = given if first else jnp.where(is_last > 0, given, up)
        saved = (saved_buf[:, cols] if first else saved_ref[micro, :, cols]).astype(jnp.float32)
        soft = jnp.tanh(saved)
        local = up * gain_ref[:, cols] * (1.0 + soft * soft)
        local_buf[:, cols] = local.astype(jnp.bfloat16)

        @pl.when(active > 0)
        def _():
            store(lo).start()

        term = jnp.sum(up * (2.0 * saved - soft), axis=0, keepdims=True)
        term = jnp.where(active > 0, term, 0.0)
        total_out[:, cols] = term if first else total_ref[:, cols] + term
        merged_ref[:, cols] = local if first else local + res_ref[:, cols]
    acc = None
    for lo in blocks:
        cols = pl.ds(lo, BLOCK)
        high, low = halves(merged_ref[:, cols])
        if first:
            both = jnp.concatenate(halves(basis_buf[cols, :]), axis=1)
            pair_ref[cols, :] = both
        else:
            both = basis_ref[cols, :]
        wide = dot(high, both, ((1,), (0,)))
        part = wide[:, :rank] + (wide[:, rank:] + dot(low, both[:, :rank], ((1,), (0,))))
        acc = part if acc is None else acc + part
    partial_ref[...] = acc

    @pl.when(active > 0)
    def _():
        for lo in blocks:
            store(lo).wait()


def front(stage, info, m, q, residue, grad, saved, gain, basis, total, sent):
    micros, rows, width = saved.shape
    first = stage == 0
    has_grad = stage < micros
    rank = basis.shape[1] if first else basis.shape[1] // 2
    whole, anywhere = pl.BlockSpec(memory_space=VMEM), pl.BlockSpec(memory_space=pl.ANY)
    outside = anywhere
    streamed = outside if first else whole
    args, specs = [info], [pl.BlockSpec(memory_space=pltpu.SMEM)]
    scratch = [pltpu.VMEM((rows, width), jnp.bfloat16), pltpu.SemaphoreType.DMA((width // BLOCK,))]
    if not first:
        args += [m, q, residue]
        specs += [whole] * 3
    if has_grad:
        args += [grad]
        specs += [outside]
        scratch += [pltpu.VMEM((rows, width), jnp.bfloat16)]
    args += [saved, gain, basis]
    specs += [streamed, whole, streamed]
    shapes = [
        jax.ShapeDtypeStruct((rows, rank), jnp.float32),
        jax.ShapeDtypeStruct((rows, width), jnp.float32),
        jax.ShapeDtypeStruct((1, width), jnp.float32),
    ]
    if first:
        scratch += [pltpu.VMEM((rows, width), jnp.bfloat16), pltpu.VMEM((width, rank), jnp.float32)]
        shapes.append(jax.ShapeDtypeStruct((width, 2 * rank), jnp.bfloat16))
    else:
        args += [total, sent]
        specs += [whole, anywhere]
    shapes.append(jax.ShapeDtypeStruct(saved.shape, jnp.bfloat16))
    if has_grad:
        scratch += [pltpu.SemaphoreType.DMA((3, width // BLOCK))]
    return pl.pallas_call(
        functools.partial(front_kernel, stage, has_grad),
        out_shape=tuple(shapes),
        in_specs=specs,
        out_specs=[whole] * (len(shapes) - 1) + [anywhere],
        input_output_aliases={} if first else {len(args) - 1: len(shapes) - 1},
        scratch_shapes=scratch,
        compiler_params=pltpu.CompilerParams(vmem_limit_bytes=24 << 20),
        cost_estimate=pl.CostEstimate(
            flops=12 * rows * width * rank, bytes_accessed=4 << 20, transcendentals=rows * width
        ),
        name="front",
    )(*args)


def factor_kernel(proj_ref, merged_ref, out_ref):
    turned = proj_ref[...].T
    high, low = halves(turned)
    for lo in range(0, merged_ref.shape[1], BLOCK):
        cols = pl.ds(lo, BLOCK)
        out_ref[:, cols] = product((high, low), halves(merged_ref[:, cols]))


def factor(proj, merged):
    rank, width = proj.shape[1], merged.shape[1]
    return pl.pallas_call(
        factor_kernel,
        out_shape=jax.ShapeDtypeStruct((rank, width), jnp.float32),
        in_specs=[pl.BlockSpec(memory_space=VMEM)] * 2,
        out_specs=pl.BlockSpec(memory_space=VMEM),
        compiler_params=pltpu.CompilerParams(vmem_limit_bytes=16 << 20),
        cost_estimate=pl.CostEstimate(
            flops=6 * rank * width * proj.shape[0], bytes_accessed=2 << 20, transcendentals=0
        ),
        name="factor",
    )(proj, merged)


def spread(array, col):
    return jnp.broadcast_to(array[:, col : col + 1], array.shape)


def repeated(array, row):
    return jnp.broadcast_to(array[row : row + 1], array.shape)


def eliminate_below(grid_ref, lower_ref):
    size = grid_ref.shape[0]
    lane = lax.broadcasted_iota(jnp.int32, (PANEL, size), 1)
    row = lax.broadcasted_iota(jnp.int32, (PANEL, size), 0)
    for lo in range(0, size, PANEL):
        band = grid_ref[lo : lo + PANEL, :]
        inside = (lane >= lo) & (lane < lo + PANEL)
        upto = lane < lo + PANEL
        cols = [spread(band, lo + j) for j in range(PANEL)]
        work = jnp.where(inside, jnp.where(lane - lo == row, 1.0, 0.0), band)
        lower_ref[lo : lo + PANEL, :] = jnp.where(upto, work, 0.0)
        for j in range(PANEL):
            here = row == j
            scaled = jnp.where(here, -1.0, cols[j]) * (1.0 / repeated(cols[j], j))
            for q in range(j + 1, PANEL):
                cols[q] = jnp.where(here, 0.0, cols[q]) - scaled * repeated(cols[q], j)
            work = jnp.where(here, 0.0, work) - scaled * repeated(work, j)
        for at in range(lo + PANEL, size, PANEL):
            other = grid_ref[at : at + PANEL, :]
            sums = [spread(other, lo + j) * repeated(work, j) for j in range(4)]
            for j in range(4, PANEL):
                sums[j % 4] += spread(other, lo + j) * repeated(work, j)
            taken = (sums[0] + sums[1]) + (sums[2] + sums[3])
            grid_ref[at : at + PANEL, :] = jnp.where(inside, 0.0, other) - taken
        grid_ref[lo : lo + PANEL, :] = jnp.where(upto, work, 0.0)


def solve_kernel(proj_ref, out_ref, grid_ref, lower_ref):
    proj = proj_ref[...]
    grid_ref[...] = dot(proj, proj, ((0,), (0,)), HIGHEST)
    eliminate_below(grid_ref, lower_ref)
    turned = dot(proj, lower_ref[...], ((1,), (1,)), HIGHEST)
    out_ref[...] = dot(turned, grid_ref[...], ((1,), (0,)), HIGHEST)


def solve(proj):
    rows, rank = proj.shape
    return pl.pallas_call(
        solve_kernel,
        out_shape=jax.ShapeDtypeStruct((rows, rank), jnp.float32),
        in_specs=[pl.BlockSpec(memory_space=VMEM)],
        out_specs=pl.BlockSpec(memory_space=VMEM),
        scratch_shapes=[pltpu.VMEM((rank, rank), jnp.float32)] * 2,
        compiler_params=pltpu.CompilerParams(vmem_limit_bytes=16 << 20),
        cost_estimate=pl.CostEstimate(
            flops=3 << 30, bytes_accessed=1 << 18, transcendentals=0
        ),
        name="solve",
    )(proj)


def back_kernel(info, merged_ref, m_ref, q_ref, *refs):
    res_ref, last_ref, sems = refs[-3:]

    def store(lo):
        cols = pl.ds(lo, BLOCK)
        return pltpu.make_async_copy(
            res_ref.at[:, cols], last_ref.at[:, cols], sems.at[lo // BLOCK]
        )

    @pl.when(info[1] > 0)
    def _():
        pair_m = halves(m_ref[...])
        for lo in range(0, merged_ref.shape[1], BLOCK):
            cols = pl.ds(lo, BLOCK)
            res_ref[:, cols] = merged_ref[:, cols] - product(pair_m, halves(q_ref[:, cols]))

            @pl.when(info[0] == info[3])
            def _():
                store(lo).start()

        @pl.when(info[0] == info[3])
        def _():
            for lo in range(0, merged_ref.shape[1], BLOCK):
                store(lo).wait()

    @pl.when(info[1] == 0)
    def _():
        res_ref[...] = jnp.zeros_like(res_ref)


def back(info, merged, m, q, last):
    rows, width = merged.shape
    anywhere = pl.BlockSpec(memory_space=pl.ANY)
    held = [] if last is None else [last]
    return pl.pallas_call(
        back_kernel,
        out_shape=(jax.ShapeDtypeStruct((rows, width), jnp.float32),) * 2,
        in_specs=[pl.BlockSpec(memory_space=pltpu.SMEM)]
        + [pl.BlockSpec(memory_space=VMEM)] * 3
        + [anywhere] * len(held),
        out_specs=[pl.BlockSpec(memory_space=VMEM), anywhere],
        input_output_aliases={4: 1} if held else {},
        scratch_shapes=[pltpu.SemaphoreType.DMA((width // BLOCK,))],
        compiler_params=pltpu.CompilerParams(vmem_limit_bytes=16 << 20),
        cost_estimate=pl.CostEstimate(
            flops=6 * rows * width * m.shape[1], bytes_accessed=3 << 20, transcendentals=0
        ),
        name="back",
    )(info, merged, m, q, *held)


def scattered_sum(array, axis):
    size = lax.axis_size(axis)
    rows, cols = array.shape
    return jnp.sum(lax.all_to_all(array.reshape(size, rows // size, cols), axis, 0, 0), axis=0)


def gathered(chunk, axis):
    size = lax.axis_size(axis)
    rows, cols = chunk.shape
    copies = jnp.broadcast_to(chunk[None], (size, rows, cols))
    return lax.all_to_all(copies, axis, 0, 0).reshape(size * rows, cols)


def partner_sum(array, axis, distances):
    if not distances:
        return array
    apart = distances.pop(0)
    pairs = [(i, i ^ apart) for i in range(lax.axis_size(axis))]
    return array + lax.ppermute(array, axis, pairs)


def body(section_inputs, out_grad, layer_gain, init_factor):
    sections = lax.axis_size("section")
    section = lax.axis_index("section")
    micros, rows, width = section_inputs.shape[1:]
    saved = section_inputs[0]
    basis = init_factor[0]
    m = q = residue = total = sent = last = None
    doublings = lax.axis_size("dp").bit_length() - 1
    distances = [1 << bit for bit in reversed(range(doublings))]
    is_last = (section == sections - 1).astype(jnp.int32)

    for stage in range(sections + micros - 1):
        micro = stage - (sections - 1 - section)
        active = ((micro >= 0) & (micro < micros)).astype(jnp.int32)
        info = jnp.stack([jnp.clip(micro, 0, micros - 1), active, is_last, jnp.int32(micros - 1)])
        partial, merged, total, *pair, sent = front(
            stage, info, m, q, residue, out_grad, saved, layer_gain, basis, total, sent
        )
        if pair:
            basis = pair[0]
        pairs = [
            (s, s - 1)
            for s in range(1, sections)
            if 0 <= stage - (sections - 1 - s) < micros
        ]
        tie = lax.optimization_barrier if not pairs else lambda both: both
        rounds = [] if pairs else list(distances)
        if not pairs:
            total = total.reshape(8, width // 8)
        chunk = scattered_sum(partial, "tensor")
        total, chunk = tie((partner_sum(total, "dp", rounds), chunk))
        proj = gathered(chunk, "tensor")
        total, proj = tie((partner_sum(total, "dp", rounds), proj))
        own_q = factor(proj, merged)
        if pairs:
            q = lax.ppermute(own_q, "section", pairs)
        own_m = solve(proj)
        total, own_m = tie((partner_sum(total, "dp", rounds), own_m))
        if pairs:
            m = lax.ppermute(own_m, "section", pairs)
        residue, last = back(info, merged, own_m, own_q, last)
        while rounds:
            total = partner_sum(total, "dp", rounds)

    tokens = micros * rows * lax.axis_size("dp")
    gain_grad = total.reshape(1, width) * (1.0 / jnp.sqrt(jnp.float32(tokens)))
    return (sent[None], last[None], gain_grad)


def solution(mesh):
    placed = (
        P("section", None, "dp", "tensor"),
        P(None, "dp", "tensor"),
        P("section", "tensor"),
        P("section", "tensor", None),
    )
    return jax.shard_map(
        body,
        mesh=mesh,
        in_specs=placed,
        out_specs=(
            P("section", None, "dp", "tensor"),
            P("section", "dp", "tensor"),
            P("section", "tensor"),
        ),
        check_vma=False,
    )
```

```python
import functools

import jax
import jax.numpy as jnp
from jax import lax
from jax.experimental import pallas as pl
from jax.experimental.pallas import tpu as pltpu
from jax.sharding import PartitionSpec as P

HIGHEST = lax.Precision.HIGHEST
VMEM = pltpu.VMEM
PANEL = 16
BLOCK = 512


def dot(left, right, over, precision=None):
    return lax.dot_general(
        left,
        right,
        (over, ((), ())),
        preferred_element_type=jnp.float32,
        precision=precision,
    )


def halves(array):
    high = array.astype(jnp.bfloat16)
    return high, (array - high.astype(jnp.float32)).astype(jnp.bfloat16)


def product(left_pair, right_pair):
    lh, ll = left_pair
    rh, rl = right_pair
    over = ((1,), (0,))
    return dot(lh, rh, over) + (dot(ll, rh, over) + dot(lh, rl, over))


def front_kernel(stage, has_grad, info, *refs):
    refs = list(refs)
    first = stage == 0
    m_ref, q_ref, res_ref = (None,) * 3 if first else [refs.pop(0) for _ in range(3)]
    grad_ref = refs.pop(0) if has_grad else None
    saved_ref, gain_ref, basis_ref = [refs.pop(0) for _ in range(3)]
    total_ref = None if first else refs.pop(0)
    if not first:
        refs.pop(0)
    partial_ref, merged_ref, total_out = [refs.pop(0) for _ in range(3)]
    pair_ref = refs.pop(0) if first else basis_ref
    sent_ref, local_buf, sent_sems = [refs.pop(0) for _ in range(3)]
    micro, active, is_last = info[0], info[1], info[2]
    width = merged_ref.shape[1]
    rank = partial_ref.shape[1]
    blocks = range(0, width, BLOCK)
    copies = []
    if has_grad:
        grad_buf, sems = refs.pop(0), refs.pop()
        copies = [
            [pltpu.make_async_copy(
                grad_ref.at[stage, :, pl.ds(lo, BLOCK)], grad_buf.at[:, pl.ds(lo, BLOCK)],
                sems.at[0, lo // BLOCK],
            )]
            for lo in blocks
        ]
    if first:
        saved_buf, basis_buf = refs
        for lo, several in zip(blocks, copies):
            cols = pl.ds(lo, BLOCK)
            several.append(pltpu.make_async_copy(
                saved_ref.at[micro, :, cols], saved_buf.at[:, cols], sems.at[1, lo // BLOCK]
            ))
            several.append(pltpu.make_async_copy(
                basis_ref.at[cols, :], basis_buf.at[cols, :], sems.at[2, lo // BLOCK]
            ))
    for several in copies:
        for copy in several:
            copy.start()

    def store(lo):
        cols = pl.ds(lo, BLOCK)
        return pltpu.make_async_copy(
            local_buf.at[:, cols], sent_ref.at[micro, :, cols], sent_sems.at[lo // BLOCK]
        )

    pair_m = None if first else halves(m_ref[...])

    for lo in blocks:
        cols = pl.ds(lo, BLOCK)
        up = None if first else product(pair_m, halves(q_ref[:, cols]))
        if has_grad:
            for copy in copies[lo // BLOCK]:
                copy.wait()
            given = grad_buf[:, cols].astype(jnp.float32)
            up = given if first else jnp.where(is_last > 0, given, up)
        saved = (saved_buf[:, cols] if first else saved_ref[micro, :, cols]).astype(jnp.float32)
        soft = jnp.tanh(saved)
        local = up * gain_ref[:, cols] * (1.0 + soft * soft)
        local_buf[:, cols] = local.astype(jnp.bfloat16)

        @pl.when(active > 0)
        def _():
            store(lo).start()

        term = jnp.sum(up * (2.0 * saved - soft), axis=0, keepdims=True)
        term = jnp.where(active > 0, term, 0.0)
        total_out[:, cols] = term if first else total_ref[:, cols] + term
        merged_ref[:, cols] = local if first else local + res_ref[:, cols]
    acc = None
    for lo in blocks:
        cols = pl.ds(lo, BLOCK)
        high, low = halves(merged_ref[:, cols])
        if first:
            both = jnp.concatenate(halves(basis_buf[cols, :]), axis=1)
            pair_ref[cols, :] = both
        else:
            both = basis_ref[cols, :]
        wide = dot(high, both, ((1,), (0,)))
        part = wide[:, :rank] + (wide[:, rank:] + dot(low, both[:, :rank], ((1,), (0,))))
        acc = part if acc is None else acc + part
    partial_ref[...] = acc

    @pl.when(active > 0)
    def _():
        for lo in blocks:
            store(lo).wait()


def front(stage, info, m, q, residue, grad, saved, gain, basis, total, sent):
    micros, rows, width = saved.shape
    first = stage == 0
    has_grad = stage < micros
    rank = basis.shape[1] if first else basis.shape[1] // 2
    whole, anywhere = pl.BlockSpec(memory_space=VMEM), pl.BlockSpec(memory_space=pl.ANY)
    outside = anywhere
    streamed = outside if first else whole
    args, specs = [info], [pl.BlockSpec(memory_space=pltpu.SMEM)]
    scratch = [pltpu.VMEM((rows, width), jnp.bfloat16), pltpu.SemaphoreType.DMA((width // BLOCK,))]
    if not first:
        args += [m, q, residue]
        specs += [whole] * 3
    if has_grad:
        args += [grad]
        specs += [outside]
        scratch += [pltpu.VMEM((rows, width), jnp.bfloat16)]
    args += [saved, gain, basis]
    specs += [streamed, whole, streamed]
    shapes = [
        jax.ShapeDtypeStruct((rows, rank), jnp.float32),
        jax.ShapeDtypeStruct((rows, width), jnp.float32),
        jax.ShapeDtypeStruct((1, width), jnp.float32),
    ]
    if first:
        scratch += [pltpu.VMEM((rows, width), jnp.bfloat16), pltpu.VMEM((width, rank), jnp.float32)]
        shapes.append(jax.ShapeDtypeStruct((width, 2 * rank), jnp.bfloat16))
    else:
        args += [total, sent]
        specs += [whole, anywhere]
    shapes.append(jax.ShapeDtypeStruct(saved.shape, jnp.bfloat16))
    if has_grad:
        scratch += [pltpu.SemaphoreType.DMA((3, width // BLOCK))]
    return pl.pallas_call(
        functools.partial(front_kernel, stage, has_grad),
        out_shape=tuple(shapes),
        in_specs=specs,
        out_specs=[whole] * (len(shapes) - 1) + [anywhere],
        input_output_aliases={} if first else {len(args) - 1: len(shapes) - 1},
        scratch_shapes=scratch,
        compiler_params=pltpu.CompilerParams(vmem_limit_bytes=24 << 20),
        cost_estimate=pl.CostEstimate(
            flops=12 * rows * width * rank, bytes_accessed=4 << 20, transcendentals=rows * width
        ),
        name="front",
    )(*args)


def factor_kernel(proj_ref, merged_ref, out_ref):
    turned = proj_ref[...].T
    high, low = halves(turned)
    for lo in range(0, merged_ref.shape[1], BLOCK):
        cols = pl.ds(lo, BLOCK)
        out_ref[:, cols] = product((high, low), halves(merged_ref[:, cols]))


def factor(proj, merged):
    rank, width = proj.shape[1], merged.shape[1]
    return pl.pallas_call(
        factor_kernel,
        out_shape=jax.ShapeDtypeStruct((rank, width), jnp.float32),
        in_specs=[pl.BlockSpec(memory_space=VMEM)] * 2,
        out_specs=pl.BlockSpec(memory_space=VMEM),
        compiler_params=pltpu.CompilerParams(vmem_limit_bytes=16 << 20),
        cost_estimate=pl.CostEstimate(
            flops=6 * rank * width * proj.shape[0], bytes_accessed=2 << 20, transcendentals=0
        ),
        name="factor",
    )(proj, merged)


def spread(array, col):
    return jnp.broadcast_to(array[:, col : col + 1], array.shape)


def repeated(array, row):
    return jnp.broadcast_to(array[row : row + 1], array.shape)


def eliminate_below(grid_ref, lower_ref):
    size = grid_ref.shape[0]
    lane = lax.broadcasted_iota(jnp.int32, (PANEL, size), 1)
    row = lax.broadcasted_iota(jnp.int32, (PANEL, size), 0)
    for lo in range(0, size, PANEL):
        band = grid_ref[lo : lo + PANEL, :]
        inside = (lane >= lo) & (lane < lo + PANEL)
        upto = lane < lo + PANEL
        cols = [spread(band, lo + j) for j in range(PANEL)]
        work = jnp.where(inside, jnp.where(lane - lo == row, 1.0, 0.0), band)
        lower_ref[lo : lo + PANEL, :] = jnp.where(upto, work, 0.0)
        for j in range(PANEL):
            here = row == j
            scaled = jnp.where(here, -1.0, cols[j]) * (1.0 / repeated(cols[j], j))
            for q in range(j + 1, PANEL):
                cols[q] = jnp.where(here, 0.0, cols[q]) - scaled * repeated(cols[q], j)
            work = jnp.where(here, 0.0, work) - scaled * repeated(work, j)
        for at in range(lo + PANEL, size, PANEL):
            other = grid_ref[at : at + PANEL, :]
            sums = [spread(other, lo + j) * repeated(work, j) for j in range(4)]
            for j in range(4, PANEL):
                sums[j % 4] += spread(other, lo + j) * repeated(work, j)
            taken = (sums[0] + sums[1]) + (sums[2] + sums[3])
            grid_ref[at : at + PANEL, :] = jnp.where(inside, 0.0, other) - taken
        grid_ref[lo : lo + PANEL, :] = jnp.where(upto, work, 0.0)


def solve_kernel(proj_ref, out_ref, grid_ref, lower_ref):
    proj = proj_ref[...]
    grid_ref[...] = dot(proj, proj, ((0,), (0,)), HIGHEST)
    eliminate_below(grid_ref, lower_ref)
    turned = dot(proj, lower_ref[...], ((1,), (1,)), HIGHEST)
    out_ref[...] = dot(turned, grid_ref[...], ((1,), (0,)), HIGHEST)


def solve(proj):
    rows, rank = proj.shape
    return pl.pallas_call(
        solve_kernel,
        out_shape=jax.ShapeDtypeStruct((rows, rank), jnp.float32),
        in_specs=[pl.BlockSpec(memory_space=VMEM)],
        out_specs=pl.BlockSpec(memory_space=VMEM),
        scratch_shapes=[pltpu.VMEM((rank, rank), jnp.float32)] * 2,
        compiler_params=pltpu.CompilerParams(vmem_limit_bytes=16 << 20),
        cost_estimate=pl.CostEstimate(
            flops=3 << 30, bytes_accessed=1 << 18, transcendentals=0
        ),
        name="solve",
    )(proj)


def back_kernel(info, merged_ref, m_ref, q_ref, *refs):
    res_ref, last_ref, sems = refs[-3:]

    def store(lo):
        cols = pl.ds(lo, BLOCK)
        return pltpu.make_async_copy(
            res_ref.at[:, cols], last_ref.at[:, cols], sems.at[lo // BLOCK]
        )

    @pl.when(info[1] > 0)
    def _():
        pair_m = halves(m_ref[...])
        for lo in range(0, merged_ref.shape[1], BLOCK):
            cols = pl.ds(lo, BLOCK)
            res_ref[:, cols] = merged_ref[:, cols] - product(pair_m, halves(q_ref[:, cols]))

            @pl.when(info[0] == info[3])
            def _():
                store(lo).start()

        @pl.when(info[0] == info[3])
        def _():
            for lo in range(0, merged_ref.shape[1], BLOCK):
                store(lo).wait()

    @pl.when(info[1] == 0)
    def _():
        res_ref[...] = jnp.zeros_like(res_ref)


def back(info, merged, m, q, last):
    rows, width = merged.shape
    anywhere = pl.BlockSpec(memory_space=pl.ANY)
    held = [] if last is None else [last]
    return pl.pallas_call(
        back_kernel,
        out_shape=(jax.ShapeDtypeStruct((rows, width), jnp.float32),) * 2,
        in_specs=[pl.BlockSpec(memory_space=pltpu.SMEM)]
        + [pl.BlockSpec(memory_space=VMEM)] * 3
        + [anywhere] * len(held),
        out_specs=[pl.BlockSpec(memory_space=VMEM), anywhere],
        input_output_aliases={4: 1} if held else {},
        scratch_shapes=[pltpu.SemaphoreType.DMA((width // BLOCK,))],
        compiler_params=pltpu.CompilerParams(vmem_limit_bytes=16 << 20),
        cost_estimate=pl.CostEstimate(
            flops=6 * rows * width * m.shape[1], bytes_accessed=3 << 20, transcendentals=0
        ),
        name="back",
    )(info, merged, m, q, *held)


def scattered_sum(array, axis):
    size = lax.axis_size(axis)
    rows, cols = array.shape
    return jnp.sum(lax.all_to_all(array.reshape(size, rows // size, cols), axis, 0, 0), axis=0)


def gathered(chunk, axis):
    size = lax.axis_size(axis)
    rows, cols = chunk.shape
    copies = jnp.broadcast_to(chunk[None], (size, rows, cols))
    return lax.all_to_all(copies, axis, 0, 0).reshape(size * rows, cols)


def group_sum(array, axis, size):
    groups = [list(range(at, at + size)) for at in range(0, lax.axis_size(axis), size)]
    copies = jnp.broadcast_to(array[None], (size, *array.shape))
    return jnp.sum(lax.all_to_all(copies, axis, 0, 0, axis_index_groups=groups), axis=0)


def body(section_inputs, out_grad, layer_gain, init_factor):
    sections = lax.axis_size("section")
    section = lax.axis_index("section")
    micros, rows, width = section_inputs.shape[1:]
    saved = section_inputs[0]
    basis = init_factor[0]
    m = q = residue = total = sent = last = None
    replicas = lax.axis_size("dp")
    near = max(replicas // 2, 1)
    others = []
    is_last = (section == sections - 1).astype(jnp.int32)

    for stage in range(sections + micros - 1):
        micro = stage - (sections - 1 - section)
        active = ((micro >= 0) & (micro < micros)).astype(jnp.int32)
        info = jnp.stack([jnp.clip(micro, 0, micros - 1), active, is_last, jnp.int32(micros - 1)])
        partial, merged, total, *pair, sent = front(
            stage, info, m, q, residue, out_grad, saved, layer_gain, basis, total, sent
        )
        if pair:
            basis = pair[0]
        pairs = [
            (s, s - 1)
            for s in range(1, sections)
            if 0 <= stage - (sections - 1 - s) < micros
        ]
        proj = gathered(scattered_sum(partial, "tensor"), "tensor")
        if not pairs:
            total, proj = lax.optimization_barrier((total.reshape(8, width // 8), proj))
            total = group_sum(total, "dp", near)
        own_q = factor(proj, merged)
        if pairs:
            q = lax.ppermute(own_q, "section", pairs)
        own_m = solve(proj)
        if pairs:
            m = lax.ppermute(own_m, "section", pairs)
        else:
            total, own_m = lax.optimization_barrier((total, own_m))
            for apart in range(near, replicas, near):
                swaps = [(i, (i + apart) % replicas) for i in range(replicas)]
                others.append(lax.ppermute(total, "dp", swaps))
        residue, last = back(info, merged, own_m, own_q, last)

    total = sum(others, total)
    tokens = micros * rows * replicas
    gain_grad = total.reshape(1, width) * (1.0 / jnp.sqrt(jnp.float32(tokens)))
    return (sent[None], last[None], gain_grad)


def solution(mesh):
    placed = (
        P("section", None, "dp", "tensor"),
        P(None, "dp", "tensor"),
        P("section", "tensor"),
        P("section", "tensor", None),
    )
    return jax.shard_map(
        body,
        mesh=mesh,
        in_specs=placed,
        out_specs=(
            P("section", None, "dp", "tensor"),
            P("section", "dp", "tensor"),
            P("section", "tensor"),
        ),
        check_vma=False,
    )
```

```python
import functools

import jax
import jax.numpy as jnp
from jax import lax
from jax.experimental import pallas as pl
from jax.experimental.pallas import tpu as pltpu
from jax.sharding import PartitionSpec as P

HIGHEST = lax.Precision.HIGHEST
VMEM = pltpu.VMEM
PANEL = 16
BLOCK = 512


def dot(left, right, over, precision=None):
    return lax.dot_general(
        left,
        right,
        (over, ((), ())),
        preferred_element_type=jnp.float32,
        precision=precision,
    )


def halves(array):
    high = array.astype(jnp.bfloat16)
    return high, (array - high.astype(jnp.float32)).astype(jnp.bfloat16)


def product(left_pair, right_pair):
    lh, ll = left_pair
    rh, rl = right_pair
    over = ((1,), (0,))
    return dot(lh, rh, over) + (dot(ll, rh, over) + dot(lh, rl, over))


def front_kernel(stage, has_grad, info, *refs):
    refs = list(refs)
    first = stage == 0
    m_ref, q_ref, res_ref = (None,) * 3 if first else [refs.pop(0) for _ in range(3)]
    grad_ref = refs.pop(0) if has_grad else None
    saved_ref, gain_ref, basis_ref = [refs.pop(0) for _ in range(3)]
    total_ref = None if first else refs.pop(0)
    if not first:
        refs.pop(0)
    partial_ref, merged_ref, total_out = [refs.pop(0) for _ in range(3)]
    pair_ref = refs.pop(0) if first else basis_ref
    sent_ref, local_buf, sent_sems = [refs.pop(0) for _ in range(3)]
    micro, active, is_last = info[0], info[1], info[2]
    width = merged_ref.shape[1]
    rank = partial_ref.shape[1]
    blocks = range(0, width, BLOCK)
    copies = []
    if has_grad:
        grad_buf, sems = refs.pop(0), refs.pop()
        copies = [
            [pltpu.make_async_copy(
                grad_ref.at[stage, :, pl.ds(lo, BLOCK)], grad_buf.at[:, pl.ds(lo, BLOCK)],
                sems.at[0, lo // BLOCK],
            )]
            for lo in blocks
        ]
    if first:
        saved_buf, basis_buf = refs
        for lo, several in zip(blocks, copies):
            cols = pl.ds(lo, BLOCK)
            several.append(pltpu.make_async_copy(
                saved_ref.at[micro, :, cols], saved_buf.at[:, cols], sems.at[1, lo // BLOCK]
            ))
            several.append(pltpu.make_async_copy(
                basis_ref.at[cols, :], basis_buf.at[cols, :], sems.at[2, lo // BLOCK]
            ))
    for several in copies:
        for copy in several:
            copy.start()

    def store(lo):
        cols = pl.ds(lo, BLOCK)
        return pltpu.make_async_copy(
            local_buf.at[:, cols], sent_ref.at[micro, :, cols], sent_sems.at[lo // BLOCK]
        )

    pair_m = None if first else halves(m_ref[...])

    for lo in blocks:
        cols = pl.ds(lo, BLOCK)
        up = None if first else product(pair_m, halves(q_ref[:, cols]))
        if has_grad:
            for copy in copies[lo // BLOCK]:
                copy.wait()
            given = grad_buf[:, cols].astype(jnp.float32)
            up = given if first else jnp.where(is_last > 0, given, up)
        saved = (saved_buf[:, cols] if first else saved_ref[micro, :, cols]).astype(jnp.float32)
        soft = jnp.tanh(saved)
        local = up * gain_ref[:, cols] * (1.0 + soft * soft)
        local_buf[:, cols] = local.astype(jnp.bfloat16)

        @pl.when(active > 0)
        def _():
            store(lo).start()

        term = jnp.sum(up * (2.0 * saved - soft), axis=0, keepdims=True)
        term = jnp.where(active > 0, term, 0.0)
        total_out[:, cols] = term if first else total_ref[:, cols] + term
        merged_ref[:, cols] = local if first else local + res_ref[:, cols]
    acc = None
    for lo in blocks:
        cols = pl.ds(lo, BLOCK)
        high, low = halves(merged_ref[:, cols])
        if first:
            both = jnp.concatenate(halves(basis_buf[cols, :]), axis=1)
            pair_ref[cols, :] = both
        else:
            both = basis_ref[cols, :]
        wide = dot(high, both, ((1,), (0,)))
        part = wide[:, :rank] + (wide[:, rank:] + dot(low, both[:, :rank], ((1,), (0,))))
        acc = part if acc is None else acc + part
    partial_ref[...] = acc

    @pl.when(active > 0)
    def _():
        for lo in blocks:
            store(lo).wait()


def front(stage, info, m, q, residue, grad, saved, gain, basis, total, sent):
    micros, rows, width = saved.shape
    first = stage == 0
    has_grad = stage < micros
    rank = basis.shape[1] if first else basis.shape[1] // 2
    whole, anywhere = pl.BlockSpec(memory_space=VMEM), pl.BlockSpec(memory_space=pl.ANY)
    outside = anywhere
    streamed = outside if first else whole
    args, specs = [info], [pl.BlockSpec(memory_space=pltpu.SMEM)]
    scratch = [pltpu.VMEM((rows, width), jnp.bfloat16), pltpu.SemaphoreType.DMA((width // BLOCK,))]
    if not first:
        args += [m, q, residue]
        specs += [whole] * 3
    if has_grad:
        args += [grad]
        specs += [outside]
        scratch += [pltpu.VMEM((rows, width), jnp.bfloat16)]
    args += [saved, gain, basis]
    specs += [streamed, whole, streamed]
    shapes = [
        jax.ShapeDtypeStruct((rows, rank), jnp.float32),
        jax.ShapeDtypeStruct((rows, width), jnp.float32),
        jax.ShapeDtypeStruct((1, width), jnp.float32),
    ]
    if first:
        scratch += [pltpu.VMEM((rows, width), jnp.bfloat16), pltpu.VMEM((width, rank), jnp.float32)]
        shapes.append(jax.ShapeDtypeStruct((width, 2 * rank), jnp.bfloat16))
    else:
        args += [total, sent]
        specs += [whole, anywhere]
    shapes.append(jax.ShapeDtypeStruct(saved.shape, jnp.bfloat16))
    if has_grad:
        scratch += [pltpu.SemaphoreType.DMA((3, width // BLOCK))]
    return pl.pallas_call(
        functools.partial(front_kernel, stage, has_grad),
        out_shape=tuple(shapes),
        in_specs=specs,
        out_specs=[whole] * (len(shapes) - 1) + [anywhere],
        input_output_aliases={} if first else {len(args) - 1: len(shapes) - 1},
        scratch_shapes=scratch,
        compiler_params=pltpu.CompilerParams(vmem_limit_bytes=24 << 20),
        cost_estimate=pl.CostEstimate(
            flops=12 * rows * width * rank, bytes_accessed=4 << 20, transcendentals=rows * width
        ),
        name="front",
    )(*args)


def factor_kernel(proj_ref, merged_ref, out_ref):
    turned = proj_ref[...].T
    high, low = halves(turned)
    for lo in range(0, merged_ref.shape[1], BLOCK):
        cols = pl.ds(lo, BLOCK)
        out_ref[:, cols] = product((high, low), halves(merged_ref[:, cols]))


def factor(proj, merged):
    rank, width = proj.shape[1], merged.shape[1]
    return pl.pallas_call(
        factor_kernel,
        out_shape=jax.ShapeDtypeStruct((rank, width), jnp.float32),
        in_specs=[pl.BlockSpec(memory_space=VMEM)] * 2,
        out_specs=pl.BlockSpec(memory_space=VMEM),
        compiler_params=pltpu.CompilerParams(vmem_limit_bytes=16 << 20),
        cost_estimate=pl.CostEstimate(
            flops=6 * rank * width * proj.shape[0], bytes_accessed=2 << 20, transcendentals=0
        ),
        name="factor",
    )(proj, merged)


def spread(array, col):
    return jnp.broadcast_to(array[:, col : col + 1], array.shape)


def repeated(array, row):
    return jnp.broadcast_to(array[row : row + 1], array.shape)


def eliminate_below(grid_ref, lower_ref):
    size = grid_ref.shape[0]
    lane = lax.broadcasted_iota(jnp.int32, (PANEL, size), 1)
    row = lax.broadcasted_iota(jnp.int32, (PANEL, size), 0)
    for lo in range(0, size, PANEL):
        band = grid_ref[lo : lo + PANEL, :]
        inside = (lane >= lo) & (lane < lo + PANEL)
        upto = lane < lo + PANEL
        cols = [spread(band, lo + j) for j in range(PANEL)]
        work = jnp.where(inside, jnp.where(lane - lo == row, 1.0, 0.0), band)
        lower_ref[lo : lo + PANEL, :] = jnp.where(upto, work, 0.0)
        for j in range(PANEL):
            here = row == j
            scaled = jnp.where(here, -1.0, cols[j]) * (1.0 / repeated(cols[j], j))
            for q in range(j + 1, PANEL):
                cols[q] = jnp.where(here, 0.0, cols[q]) - scaled * repeated(cols[q], j)
            work = jnp.where(here, 0.0, work) - scaled * repeated(work, j)
        for at in range(lo + PANEL, size, PANEL):
            other = grid_ref[at : at + PANEL, :]
            sums = [spread(other, lo + j) * repeated(work, j) for j in range(4)]
            for j in range(4, PANEL):
                sums[j % 4] += spread(other, lo + j) * repeated(work, j)
            taken = (sums[0] + sums[1]) + (sums[2] + sums[3])
            grid_ref[at : at + PANEL, :] = jnp.where(inside, 0.0, other) - taken
        grid_ref[lo : lo + PANEL, :] = jnp.where(upto, work, 0.0)


def solve_kernel(proj_ref, out_ref, grid_ref, lower_ref):
    proj = proj_ref[...]
    grid_ref[...] = dot(proj, proj, ((0,), (0,)), HIGHEST)
    eliminate_below(grid_ref, lower_ref)
    turned = dot(proj, lower_ref[...], ((1,), (1,)), HIGHEST)
    out_ref[...] = dot(turned, grid_ref[...], ((1,), (0,)), HIGHEST)


def solve(proj):
    rows, rank = proj.shape
    return pl.pallas_call(
        solve_kernel,
        out_shape=jax.ShapeDtypeStruct((rows, rank), jnp.float32),
        in_specs=[pl.BlockSpec(memory_space=VMEM)],
        out_specs=pl.BlockSpec(memory_space=VMEM),
        scratch_shapes=[pltpu.VMEM((rank, rank), jnp.float32)] * 2,
        compiler_params=pltpu.CompilerParams(vmem_limit_bytes=16 << 20),
        cost_estimate=pl.CostEstimate(
            flops=3 << 30, bytes_accessed=1 << 18, transcendentals=0
        ),
        name="solve",
    )(proj)


def back_kernel(info, merged_ref, m_ref, q_ref, *refs):
    res_ref, last_ref, sems = refs[-3:]

    def store(lo):
        cols = pl.ds(lo, BLOCK)
        return pltpu.make_async_copy(
            res_ref.at[:, cols], last_ref.at[:, cols], sems.at[lo // BLOCK]
        )

    @pl.when(info[1] > 0)
    def _():
        pair_m = halves(m_ref[...])
        for lo in range(0, merged_ref.shape[1], BLOCK):
            cols = pl.ds(lo, BLOCK)
            res_ref[:, cols] = merged_ref[:, cols] - product(pair_m, halves(q_ref[:, cols]))

            @pl.when(info[0] == info[3])
            def _():
                store(lo).start()

        @pl.when(info[0] == info[3])
        def _():
            for lo in range(0, merged_ref.shape[1], BLOCK):
                store(lo).wait()

    @pl.when(info[1] == 0)
    def _():
        res_ref[...] = jnp.zeros_like(res_ref)


def back(info, merged, m, q, last):
    rows, width = merged.shape
    anywhere = pl.BlockSpec(memory_space=pl.ANY)
    held = [] if last is None else [last]
    return pl.pallas_call(
        back_kernel,
        out_shape=(jax.ShapeDtypeStruct((rows, width), jnp.float32),) * 2,
        in_specs=[pl.BlockSpec(memory_space=pltpu.SMEM)]
        + [pl.BlockSpec(memory_space=VMEM)] * 3
        + [anywhere] * len(held),
        out_specs=[pl.BlockSpec(memory_space=VMEM), anywhere],
        input_output_aliases={4: 1} if held else {},
        scratch_shapes=[pltpu.SemaphoreType.DMA((width // BLOCK,))],
        compiler_params=pltpu.CompilerParams(vmem_limit_bytes=16 << 20),
        cost_estimate=pl.CostEstimate(
            flops=6 * rows * width * m.shape[1], bytes_accessed=3 << 20, transcendentals=0
        ),
        name="back",
    )(info, merged, m, q, *held)


def scattered_sum(array, axis):
    size = lax.axis_size(axis)
    rows, cols = array.shape
    return jnp.sum(lax.all_to_all(array.reshape(size, rows // size, cols), axis, 0, 0), axis=0)


def gathered(chunk, axis):
    size = lax.axis_size(axis)
    rows, cols = chunk.shape
    copies = jnp.broadcast_to(chunk[None], (size, rows, cols))
    return lax.all_to_all(copies, axis, 0, 0).reshape(size * rows, cols)


def group_sum(array, axis, size):
    groups = [list(range(at, at + size)) for at in range(0, lax.axis_size(axis), size)]
    copies = jnp.broadcast_to(array[None], (size, *array.shape))
    return jnp.sum(lax.all_to_all(copies, axis, 0, 0, axis_index_groups=groups), axis=0)


def body(section_inputs, out_grad, layer_gain, init_factor):
    sections = lax.axis_size("section")
    section = lax.axis_index("section")
    micros, rows, width = section_inputs.shape[1:]
    saved = section_inputs[0]
    basis = init_factor[0]
    m = q = residue = total = sent = last = None
    replicas = lax.axis_size("dp")
    near = max(replicas // 2, 1)
    is_last = (section == sections - 1).astype(jnp.int32)

    for stage in range(sections + micros - 1):
        micro = stage - (sections - 1 - section)
        active = ((micro >= 0) & (micro < micros)).astype(jnp.int32)
        info = jnp.stack([jnp.clip(micro, 0, micros - 1), active, is_last, jnp.int32(micros - 1)])
        partial, merged, total, *pair, sent = front(
            stage, info, m, q, residue, out_grad, saved, layer_gain, basis, total, sent
        )
        if pair:
            basis = pair[0]
        pairs = [
            (s, s - 1)
            for s in range(1, sections)
            if 0 <= stage - (sections - 1 - s) < micros
        ]
        chunk = scattered_sum(partial, "tensor")
        if not pairs:
            total = total.reshape(8, width // 8)
            others = [total]
            for apart in range(near, replicas, near):
                swaps = [(i, (i + apart) % replicas) for i in range(replicas)]
                others.append(lax.ppermute(total, "dp", swaps))
            total, chunk = lax.optimization_barrier((sum(others[1:], others[0]), chunk))
        proj = gathered(chunk, "tensor")
        if not pairs:
            total, proj = lax.optimization_barrier((total, proj))
            total = group_sum(total, "dp", near)
        own_q = factor(proj, merged)
        if pairs:
            q = lax.ppermute(own_q, "section", pairs)
        own_m = solve(proj)
        if pairs:
            m = lax.ppermute(own_m, "section", pairs)
        residue, last = back(info, merged, own_m, own_q, last)

    tokens = micros * rows * replicas
    gain_grad = total.reshape(1, width) * (1.0 / jnp.sqrt(jnp.float32(tokens)))
    return (sent[None], last[None], gain_grad)


def solution(mesh):
    placed = (
        P("section", None, "dp", "tensor"),
        P(None, "dp", "tensor"),
        P("section", "tensor"),
        P("section", "tensor", None),
    )
    return jax.shard_map(
        body,
        mesh=mesh,
        in_specs=placed,
        out_specs=(
            P("section", None, "dp", "tensor"),
            P("section", "dp", "tensor"),
            P("section", "tensor"),
        ),
        check_vma=False,
    )
```
